512 devices in a mesh: rep: 8 (over z_hi, core), fsdp: 16 (over y, z_lo), tp: 4 (over x).
Axes of the slice: x: 4, y: 8, z: 8 (z_hi: 4, z_lo: 2; z = z_hi * 2 + z_lo), core: 2. Of those that a mesh axis runs over, the one named last changes fastest.
Arguments:
- tokens: bfloat16 [32768, 8192], P(('rep', 'fsdp'), 'tp'), may hold values from -6 to 6
- cotangent: bfloat16 [32768, 1024], P(('rep', 'fsdp')), may hold values from -6 to 6
- codes: bfloat16 [8192, 1024], P('tp', 'fsdp'), may hold values from -384 to 384
- scales: bfloat16 [64, 1024], P('tp', 'fsdp'), may hold values from 8.6307526e-05 to 0.0003452301
- adapter_down: float32 [8192, 64], P('tp'), may hold values from -6 to 6
- adapter_up: float32 [64, 1024], replicated, may hold values from -6 to 6
Outputs:
- values: bfloat16 [32768, 1024], P(('rep', 'fsdp'), 'tp')
- grad_tokens: bfloat16 [32768, 8192], P(('rep', 'fsdp'), 'tp')
- refreshed_down: float32 [8192, 64], P('tp')
- scorer_a: bfloat16 [8192, 64], replicated
- refreshed_up: float32 [64, 1024], P(None, 'tp')
The draws below stay inside these ranges and needn't reach their ends.
All inputs are finite; a program needn't handle non-finite values.
Results may differ from the reference program's by a relative error of at most 0.0053.
Values may be sent and summed in bfloat16 or wider, within the bound.
No kernel may reach another device: no remote copies, remote signals or barrier semaphores. Data moves between devices by JAX's collectives and lax.ppermute only.
A program may use at most 64 MiB of HBM per device.

```python
import math
import jax
import jax.numpy as jnp
from jax import lax

MODEL_WIDTH = 8192
VALUE_WIDTH = 1024
ADAPTER_RANK = 64
QB = 128
TOKENS = 32768


def block_scale(own_key, dims, cuts, low, top_value):
    factor_of = 1.0
    for axis_at, parts in cuts:
        steps = jax.random.uniform(jax.random.fold_in(jax.random.fold_in(own_key, 6), axis_at), (parts,), jnp.float32, low / len(cuts), top_value / len(cuts))
        factor_of = factor_of * jnp.repeat(jnp.exp(steps), dims[axis_at] // parts).reshape((-1,) + (1,) * (len(dims) - 1 - axis_at))
    return factor_of


def gaussian(stream_key, shape, scale, bound, shards=(), dtype=jnp.bfloat16):
    values = jax.random.normal(stream_key, shape, jnp.float32) * scale
    if len(shards) > 0:
        values = block_scale(stream_key, shape, shards, -0.22, 0.18) * values
    return jnp.clip(values, min=-bound, max=bound).astype(dtype)


def setup_inputs(seed: int = 0) -> dict:
    key_list = jax.random.split(jax.random.key(seed), 7)
    return {
        "tokens": gaussian(key_list[0], (TOKENS, MODEL_WIDTH), 1.0, 6.0, ((0, 128), (1, 4))),
        "cotangent": gaussian(key_list[1], (TOKENS, VALUE_WIDTH), 1.0, 6.0, ((0, 128),)),
        "codes": gaussian(key_list[2], (MODEL_WIDTH, VALUE_WIDTH), 64.0, 384.0, ((0, 4), (1, 16))),
        "scales": jnp.clip(jnp.exp(math.log(0.0003452301) - 1.3862944 * jax.random.uniform(key_list[3], (MODEL_WIDTH // QB, VALUE_WIDTH), jnp.float32) ** block_scale(key_list[3], (MODEL_WIDTH // QB, VALUE_WIDTH), ((0, 4), (1, 16)), -0.2, 0.2)), 8.630752563476562e-05, 0.0003452301).astype(jnp.bfloat16),
        "adapter_down": gaussian(key_list[4], (MODEL_WIDTH, ADAPTER_RANK), 1.0, 6.0, ((0, 4),), jnp.float32),
        "adapter_up": gaussian(key_list[5], (ADAPTER_RANK, VALUE_WIDTH), 0.5, 6.0, (), jnp.float32),
    }


adapter_scale = 0.25
down_learning_rate = 1.0
up_learning_rate = 0.1
eps_norm = 1e-06

def norm_divided(grad, axis):
    return grad * lax.rsqrt(lax.optimization_barrier(jnp.mean(grad * grad, axis=axis, keepdims=True)) + eps_norm)

def reference(tokens, cotangent, codes, scales, adapter_down, adapter_up):
    inv_root = 1.0 / math.sqrt(MODEL_WIDTH)
    blocked = codes.astype(jnp.float32).reshape(MODEL_WIDTH // QB, QB, VALUE_WIDTH) * scales.astype(jnp.float32)[:, None, :]
    weight = blocked.reshape(MODEL_WIDTH, VALUE_WIDTH).astype(jnp.bfloat16)
    down_lowered = adapter_down.astype(jnp.bfloat16)
    rank_product = jnp.dot(tokens, down_lowered, preferred_element_type=jnp.float32) * inv_root
    main_part = jnp.dot(tokens, weight, preferred_element_type=jnp.float32)
    adapter_branch_output = adapter_scale * jnp.dot(rank_product, adapter_up, precision=lax.Precision.HIGHEST)
    values = (main_part + adapter_branch_output).astype(jnp.bfloat16)
    wide_cotangent = cotangent.astype(jnp.float32)
    rank_backward = adapter_scale * jnp.dot(wide_cotangent, adapter_up.T, precision=lax.Precision.HIGHEST)
    back_low = rank_backward.astype(jnp.bfloat16)
    through = jnp.einsum('tn,kn->tk', cotangent, weight, preferred_element_type=jnp.float32)
    beside = jnp.einsum('tr,kr->tk', back_low, down_lowered, preferred_element_type=jnp.float32) * inv_root
    grad_tokens = (through + beside).astype(jnp.bfloat16)
    down_gradient = jnp.einsum('tk,tr->kr', tokens, back_low, preferred_element_type=jnp.float32) * inv_root
    up_gradient = adapter_scale * jnp.dot(rank_product.T, wide_cotangent, precision=lax.Precision.HIGHEST)
    refreshed_down = adapter_down - down_learning_rate * norm_divided(down_gradient, 1)
    refreshed_up = adapter_up - up_learning_rate * norm_divided(up_gradient, 0)
    return (values, grad_tokens, refreshed_down, refreshed_down.astype(jnp.bfloat16), refreshed_up)
```

```python
import math

import jax
import jax.numpy as jnp
from jax import lax
from jax.experimental import pallas as pl
from jax.experimental.pallas import tpu as pltpu
from jax.sharding import Mesh
from jax.sharding import PartitionSpec as P

MODEL_WIDTH = 8192
QB = 128
INV_ROOT = 1.0 / math.sqrt(MODEL_WIDTH)

adapter_scale = 0.25
down_learning_rate = 1.0
up_learning_rate = 0.1
eps_norm = 1e-06

f32 = jnp.float32
bf16 = jnp.bfloat16
PLANE = ("zh", "y", "zl")
LIMIT = 48 * 1024 * 1024

NN = (((1,), (0,)), ((), ()))
NT = (((1,), (1,)), ((), ()))
TN = (((0,), (0,)), ((), ()))


def dot(a, b, dims):
    return lax.dot_general(a, b, dims, preferred_element_type=f32)


def thirds(a):
    high = a.astype(bf16)
    rest = a - high.astype(f32)
    middle = rest.astype(bf16)
    return high, middle, (rest - middle.astype(f32)).astype(bf16)


def call(kernel, outs, scalars, arrays, flops=0):
    return pl.pallas_call(
        kernel,
        out_shape=outs,
        in_specs=[pl.BlockSpec(memory_space=pltpu.SMEM)] * len(scalars)
        + [pl.BlockSpec(memory_space=pltpu.VMEM)] * len(arrays),
        out_specs=jax.tree.map(lambda _: pl.BlockSpec(memory_space=pltpu.VMEM), outs),
        compiler_params=pltpu.CompilerParams(vmem_limit_bytes=LIMIT),
        cost_estimate=pl.CostEstimate(flops=flops, bytes_accessed=1 << 20, transcendentals=0),
    )(*scalars, *arrays)


def shape(*dims, dtype=f32):
    return jax.ShapeDtypeStruct(dims, dtype)


def halves(core, width):
    first = pl.multiple_of(core * width, width)
    return pl.ds(first, width), pl.ds(pl.multiple_of(width - first, width), width)


def store_tiles(ref, wide):
    rows, columns = wide.shape[0] // 8, wide.shape[1] // 128
    for i in range(rows):
        for j in range(columns):
            ref[i * columns + j] = wide[8 * i : 8 * i + 8, 128 * j : 128 * j + 128]


def load_tiles(ref, first, columns):
    rows = [
        jnp.concatenate([ref[i * columns + j, first : first + 8] for j in range(columns)], axis=1)
        for i in range(8)
    ]
    return jnp.concatenate(rows, axis=0)


def down_gradient_kernel(core, tokens, cotangent, up, low_ref, keep_ref, send_ref):
    high, middle, low = thirds(up[...])
    wide = cotangent[...]
    back = dot(wide, low, NT) + dot(wide, middle, NT) + dot(wide, high, NT)
    back_low = (adapter_scale * back).astype(bf16)
    low_ref[...] = back_low
    own, other = halves(core[0], tokens.shape[1] // 2)
    store_tiles(send_ref, dot(back_low, tokens[:, other], TN) * INV_ROOT)
    store_tiles(keep_ref, dot(back_low, tokens[:, own], TN) * INV_ROOT)


def up_gradient_kernel(tokens, down, cotangent, rank_ref, tiles_ref):
    rank = dot(tokens[...], down[...].astype(bf16), NT) * INV_ROOT
    rank_ref[...] = rank
    high, middle, low = thirds(rank)
    wide = cotangent[...]
    store_tiles(
        tiles_ref, adapter_scale * (dot(low, wide, TN) + dot(middle, wide, TN) + dot(high, wide, TN))
    )


def total_kernel(parts, out):
    total = parts[0]
    for i in range(1, parts.shape[0]):
        total = total + parts[i]
    for i in range(parts.shape[0]):
        out[i] = total


def normed(grad):
    mean = jnp.mean(grad * grad, axis=0, keepdims=True)
    return grad * lax.rsqrt(mean + eps_norm)


def scorer_kernel(core, gathered, down, out, raw_ref):
    own, _ = halves(core[0], down.shape[1] // 2)
    grad = load_tiles(gathered, 0, 8)
    raw_ref[...] = grad
    fresh = (down[:, own] - down_learning_rate * normed(grad)).astype(bf16)
    up_grad = load_tiles(gathered, 8, 8).astype(bf16)
    for p in range(4):
        out[p, :, :1024] = fresh
        out[p, :, 1024:] = up_grad[:, 256 * p : 256 * p + 256]


def down_kernel(core, raw, raw_other, down, out):
    own, other = halves(core[0], down.shape[1] // 2)
    out[:, own] = down[:, own] - down_learning_rate * normed(raw[...])
    out[:, other] = down[:, other] - down_learning_rate * normed(raw_other[...])


def finish_kernel(core, place, rows, rows_other, part, part_other, up, scorer_ref, up_ref):
    first = core[0] == 0
    for p in range(4):
        mine, theirs = rows[p], rows_other[p]
        scorer_ref[2048 * p : 2048 * p + 1024, :] = jnp.where(first, mine, theirs).T
        scorer_ref[2048 * p + 1024 : 2048 * p + 2048, :] = jnp.where(first, theirs, mine).T
    columns = pl.ds(pl.multiple_of(place[0] * 256, 256), 256)
    up_ref[...] = up[:, columns] - up_learning_rate * normed(part[...] + part_other[...])


def near_values_kernel(core, tokens, weight, rank, up, out):
    own, _ = halves(core[0], tokens.shape[1] // 2)
    branch = lax.dot_general(
        rank[...], up[...], NN, precision=lax.Precision.HIGHEST, preferred_element_type=f32
    )
    out[...] = dot(tokens[:, own], weight[...], NT) + adapter_scale * branch


def far_values_kernel(core, tokens, weight, near, out):
    _, other = halves(core[0], tokens.shape[1] // 2)
    whole = near[...] + dot(tokens[:, other], weight[...], NT)
    for p in range(4):
        out[p] = whole[:, 256 * p : 256 * p + 256]


def token_gradient_kernel(core, cotangent, near, far, back_low, down, out):
    own, other = halves(core[0], down.shape[1] // 2)
    for place, weight in ((own, near), (other, far)):
        beside = dot(back_low[...], down[:, place].astype(bf16), NN) * INV_ROOT
        out[:, place] = (dot(cotangent[...], weight[...], NN) + beside).astype(bf16)


def body(tokens, cotangent, codes, scales, adapter_down, adapter_up):
    core_at = lax.axis_index("c")
    core = core_at.astype(jnp.int32).reshape(1)
    place = lax.axis_index("x").astype(jnp.int32).reshape(1)
    down = adapter_down.T
    swap = [(0, 1), (1, 0)]
    half = codes.shape[0] // 2

    with jax.named_scope("dequant"):
        code_half = lax.dynamic_slice_in_dim(codes.T, core_at * half, half, 1)
        scale_half = lax.dynamic_slice_in_dim(scales.T, core_at * (half // QB), half // QB, 1)
        blocked = code_half.astype(f32).reshape(-1, half // QB, QB) * scale_half.astype(f32)[:, :, None]
        mine = blocked.reshape(code_half.shape).astype(bf16)
        theirs = lax.ppermute(mine, "zl", swap)
        low_first = lax.axis_index("zl") == 0
        pair = jnp.concatenate(
            [jnp.where(low_first, mine, theirs), jnp.where(low_first, theirs, mine)], axis=0
        )
    with jax.named_scope("weight_gather"):
        near = lax.all_gather(pair, "y", axis=0, tiled=True)
        far = lax.ppermute(near, "c", swap)

    with jax.named_scope("gradients"):
        back_low, keep, send = call(
            down_gradient_kernel,
            (shape(256, 64, dtype=bf16), shape(64, 8, 128), shape(64, 8, 128)),
            (core,),
            (tokens, cotangent, adapter_up),
        )
        arrived = lax.ppermute(send, "c", swap)
        rank, up_tiles = call(
            up_gradient_kernel, (shape(256, 64), shape(64, 8, 128)), (), (tokens, down, cotangent)
        )
    with jax.named_scope("plane_sum"):
        parts = jnp.concatenate([keep + arrived, up_tiles], axis=1)
        parts = lax.all_to_all(parts, PLANE, 0, 0, tiled=True)
        total = call(total_kernel, shape(64, 16, 128), (), (parts,))
        gathered = lax.all_to_all(total, PLANE, 0, 0, tiled=True)
    with jax.named_scope("refresh"):
        rows, raw = call(
            scorer_kernel, (shape(4, 64, 1280, dtype=bf16), shape(64, 1024)), (core,), (gathered, down)
        )
        raw_other = lax.ppermute(raw, "c", swap)
        rows = lax.all_to_all(rows, "x", 0, 0, tiled=True)
        part = jnp.sum(rows[:, :, 1024:].astype(f32), axis=0)
        rows = rows[:, :, :1024]
        rows_other = lax.ppermute(rows, "c", swap)
        part_other = lax.ppermute(part, "c", swap)
        refreshed_down = call(
            down_kernel, shape(64, 2048), (core,), (raw, raw_other, down)
        ).T
        scorer_a, refreshed_up = call(
            finish_kernel,
            (shape(8192, 64, dtype=bf16), shape(64, 256)),
            (core, place),
            (rows, rows_other, part, part_other, adapter_up),
        )
    with jax.named_scope("values"):
        near_part = call(
            near_values_kernel, shape(256, 1024), (core,), (tokens, near, rank, adapter_up)
        )
        whole = call(far_values_kernel, shape(4, 256, 256), (core,), (tokens, far, near_part))
        at = lax.axis_index("x")
        values = lax.dynamic_index_in_dim(whole, at, 0, keepdims=False)
        for k in range(1, 4):
            out = lax.dynamic_index_in_dim(whole, (at + k) % 4, 0, keepdims=False)
            values = values + lax.ppermute(out, "x", [(i, (i + k) % 4) for i in range(4)])
        values = values.astype(bf16)
    with jax.named_scope("grad_tokens"):
        grad_tokens = call(
            token_gradient_kernel,
            shape(256, 2048, dtype=bf16),
            (core,),
            (cotangent, near, far, back_low, down),
        )
    return (values, grad_tokens, refreshed_down, scorer_a, refreshed_up)


def solution(mesh):
    fine = Mesh(mesh.devices.reshape(4, 2, 8, 2, 4), ("zh", "c", "y", "zl", "x"))
    tokens_at = ("zh", "c", "y", "zl")
    in_specs = (
        P(tokens_at, "x"),
        P(tokens_at, None),
        P("x", ("y", "zl")),
        P("x", ("y", "zl")),
        P("x", None),
        P(),
    )
    out_specs = (
        P(tokens_at, "x"),
        P(tokens_at, "x"),
        P("x", None),
        P(),
        P(None, "x"),
    )
    return jax.shard_map(body, mesh=fine, in_specs=in_specs, out_specs=out_specs, check_vma=False)
```

```python
import math

import jax
import jax.numpy as jnp
from jax import lax
from jax.experimental import pallas as pl
from jax.experimental.pallas import tpu as pltpu
from jax.sharding import Mesh
from jax.sharding import PartitionSpec as P

MODEL_WIDTH = 8192
QB = 128
INV_ROOT = 1.0 / math.sqrt(MODEL_WIDTH)

adapter_scale = 0.25
down_learning_rate = 1.0
up_learning_rate = 0.1
eps_norm = 1e-06

f32 = jnp.float32
bf16 = jnp.bfloat16
PLANE = ("zh", "y", "zl")
LIMIT = 48 * 1024 * 1024

NN = (((1,), (0,)), ((), ()))
NT = (((1,), (1,)), ((), ()))
TN = (((0,), (0,)), ((), ()))


def dot(a, b, dims):
    return lax.dot_general(a, b, dims, preferred_element_type=f32)


def thirds(a):
    high = a.astype(bf16)
    rest = a - high.astype(f32)
    middle = rest.astype(bf16)
    return high, middle, (rest - middle.astype(f32)).astype(bf16)


def call(kernel, outs, scalars, arrays, flops=0):
    return pl.pallas_call(
        kernel,
        out_shape=outs,
        in_specs=[pl.BlockSpec(memory_space=pltpu.SMEM)] * len(scalars)
        + [pl.BlockSpec(memory_space=pltpu.VMEM)] * len(arrays),
        out_specs=jax.tree.map(lambda _: pl.BlockSpec(memory_space=pltpu.VMEM), outs),
        compiler_params=pltpu.CompilerParams(vmem_limit_bytes=LIMIT),
        cost_estimate=pl.CostEstimate(flops=flops, bytes_accessed=1 << 20, transcendentals=0),
    )(*scalars, *arrays)


def shape(*dims, dtype=f32):
    return jax.ShapeDtypeStruct(dims, dtype)


def halves(core, width):
    first = pl.multiple_of(core * width, width)
    return pl.ds(first, width), pl.ds(pl.multiple_of(width - first, width), width)


def store_tiles(ref, wide):
    rows, columns = wide.shape[0] // 8, wide.shape[1] // 128
    for i in range(rows):
        for j in range(columns):
            ref[i * columns + j] = wide[8 * i : 8 * i + 8, 128 * j : 128 * j + 128]


def load_tiles(ref, first, columns):
    rows = [
        jnp.concatenate([ref[i * columns + j, first : first + 8] for j in range(columns)], axis=1)
        for i in range(8)
    ]
    return jnp.concatenate(rows, axis=0)


def down_gradient_kernel(core, tokens, cotangent, up, low_ref, keep_ref, send_ref):
    high, middle, low = thirds(up[...])
    wide = cotangent[...]
    back = dot(wide, low, NT) + dot(wide, middle, NT) + dot(wide, high, NT)
    back_low = (adapter_scale * back).astype(bf16)
    low_ref[...] = back_low
    own, other = halves(core[0], tokens.shape[1] // 2)
    store_tiles(send_ref, dot(back_low, tokens[:, other], TN) * INV_ROOT)
    store_tiles(keep_ref, dot(back_low, tokens[:, own], TN) * INV_ROOT)


def up_gradient_kernel(tokens, down, cotangent, rank_ref, tiles_ref):
    rank = dot(tokens[...], down[...].astype(bf16), NT) * INV_ROOT
    rank_ref[...] = rank
    high, middle, low = thirds(rank)
    wide = cotangent[...]
    store_tiles(
        tiles_ref, adapter_scale * (dot(low, wide, TN) + dot(middle, wide, TN) + dot(high, wide, TN))
    )


def total_kernel(parts, out):
    total = parts[0]
    for i in range(1, parts.shape[0]):
        total = total + parts[i]
    for i in range(parts.shape[0]):
        out[i] = total


def normed(grad):
    mean = jnp.mean(grad * grad, axis=0, keepdims=True)
    return grad * lax.rsqrt(mean + eps_norm)


def scorer_kernel(core, gathered, down, out, raw_ref):
    own, _ = halves(core[0], down.shape[1] // 2)
    grad = load_tiles(gathered, 0, 8)
    raw_ref[...] = grad
    fresh = (down[:, own] - down_learning_rate * normed(grad)).astype(bf16)
    up_grad = load_tiles(gathered, 8, 8).astype(bf16)
    for p in range(4):
        out[p, :64, :] = fresh
        for i in range(4):
            out[p, 64:, 256 * i : 256 * i + 256] = up_grad[
                16 * i : 16 * i + 16, 256 * p : 256 * p + 256
            ]


def down_kernel(core, raw, raw_other, down, out):
    own, other = halves(core[0], down.shape[1] // 2)
    out[:, own] = down[:, own] - down_learning_rate * normed(raw[...])
    out[:, other] = down[:, other] - down_learning_rate * normed(raw_other[...])


def part_sum(rows):
    wide = rows[0, 64:, :].astype(f32)
    for p in range(1, 4):
        wide = wide + rows[p, 64:, :].astype(f32)
    return jnp.concatenate([wide[:, 256 * i : 256 * i + 256] for i in range(4)], axis=0)


def finish_kernel(core, place, rows, rows_other, up, scorer_ref, up_ref):
    own, other = halves(core[0], 1024)
    for p in range(4):
        scorer_ref[:, pl.ds(pl.multiple_of(2048 * p + own.start, 1024), 1024)] = rows[p, :64, :]
        scorer_ref[:, pl.ds(pl.multiple_of(2048 * p + other.start, 1024), 1024)] = rows_other[p, :64, :]
    columns = pl.ds(pl.multiple_of(place[0] * 256, 256), 256)
    total = part_sum(rows) + part_sum(rows_other)
    up_ref[...] = up[:, columns] - up_learning_rate * normed(total)


def near_values_kernel(core, tokens, weight, rank, up, out):
    own, _ = halves(core[0], tokens.shape[1] // 2)
    branch = lax.dot_general(
        rank[...], up[...], NN, precision=lax.Precision.HIGHEST, preferred_element_type=f32
    )
    out[...] = dot(tokens[:, own], weight[...], NT) + adapter_scale * branch


def far_values_kernel(core, place, tokens, weight, near, kept, *sent):
    _, other = halves(core[0], tokens.shape[1] // 2)
    far_tokens = tokens[:, other]
    for k, ref in enumerate((kept, *sent)):
        first = pl.multiple_of(lax.rem(place[0] + k, 4) * 256, 256)
        columns = pl.ds(first, 256)
        ref[...] = near[:, columns] + dot(far_tokens, weight[columns, :], NT)


def sum_values_kernel(*refs):
    *parts, out = refs
    out[...] = (parts[0][...] + parts[1][...] + parts[2][...] + parts[3][...]).astype(bf16)


def tie_kernel(value, before, out):
    del value, before, out


def tie(value, before):
    anywhere = pl.BlockSpec(memory_space=pl.ANY)
    return pl.pallas_call(
        tie_kernel,
        out_shape=jax.ShapeDtypeStruct(value.shape, value.dtype),
        in_specs=[anywhere, anywhere],
        out_specs=anywhere,
        input_output_aliases={0: 0},
    )(value, before)


def token_gradient_kernel(core, cotangent, near, far, back_low, down, out):
    own, other = halves(core[0], down.shape[1] // 2)
    for place, weight in ((own, near), (other, far)):
        beside = dot(back_low[...], down[:, place].astype(bf16), NN) * INV_ROOT
        out[:, place] = (dot(cotangent[...], weight[...], NN) + beside).astype(bf16)


def body(tokens, cotangent, codes, scales, adapter_down, adapter_up):
    core_at = lax.axis_index("c")
    core = core_at.astype(jnp.int32).reshape(1)
    place = lax.axis_index("x").astype(jnp.int32).reshape(1)
    down = adapter_down.T
    swap = [(0, 1), (1, 0)]
    half = codes.shape[0] // 2

    with jax.named_scope("dequant"):
        code_half = lax.dynamic_slice_in_dim(codes.T, core_at * half, half, 1)
        scale_half = lax.dynamic_slice_in_dim(scales.T, core_at * (half // QB), half // QB, 1)
        blocked = code_half.astype(f32).reshape(-1, half // QB, QB) * scale_half.astype(f32)[:, :, None]
        mine = blocked.reshape(code_half.shape).astype(bf16)
        theirs = lax.ppermute(mine, "zl", swap)
        low_first = lax.axis_index("zl") == 0
        pair = jnp.concatenate(
            [jnp.where(low_first, mine, theirs), jnp.where(low_first, theirs, mine)], axis=0
        )
    with jax.named_scope("weight_gather"):
        near = lax.all_gather(pair, "y", axis=0, tiled=True)

    with jax.named_scope("gradients"):
        back_low, keep, send = call(
            down_gradient_kernel,
            (shape(256, 64, dtype=bf16), shape(64, 8, 128), shape(64, 8, 128)),
            (core,),
            (tokens, cotangent, adapter_up),
        )
        arrived = lax.ppermute(send, "c", swap)
        rank, up_tiles = call(
            up_gradient_kernel, (shape(256, 64), shape(64, 8, 128)), (), (tokens, down, cotangent)
        )
    with jax.named_scope("plane_sum"):
        parts = jnp.concatenate([keep + arrived, up_tiles], axis=1)
        parts = lax.all_to_all(parts, PLANE, 0, 0, tiled=True)
        total = call(total_kernel, shape(64, 16, 128), (), (parts,))
        gathered = lax.all_to_all(total, PLANE, 0, 0, tiled=True)
    with jax.named_scope("weight_swap"):
        near = tie(near, gathered)
        far = lax.ppermute(near, "c", swap)
    with jax.named_scope("refresh"):
        rows, raw = call(
            scorer_kernel, (shape(4, 80, 1024, dtype=bf16), shape(64, 1024)), (core,), (gathered, down)
        )
        raw_other = lax.ppermute(raw, "c", swap)
        rows = lax.all_to_all(rows, "x", 0, 0, tiled=True)
        rows_other = lax.ppermute(rows, "c", swap)
        refreshed_down = call(
            down_kernel, shape(64, 2048), (core,), (raw, raw_other, down)
        ).T
        scorer_a, refreshed_up = call(
            finish_kernel,
            (shape(64, 8192, dtype=bf16), shape(64, 256)),
            (core, place),
            (rows, rows_other, adapter_up),
        )
        scorer_a = scorer_a.T
    with jax.named_scope("values"):
        near_part = call(
            near_values_kernel, shape(256, 1024), (core,), (tokens, near, rank, adapter_up)
        )
        kept, *sent = call(
            far_values_kernel,
            (shape(256, 256),) * 4,
            (core, place),
            (tokens, far, near_part),
        )
        came = [
            lax.ppermute(part, "x", [(i, (i + k) % 4) for i in range(4)])
            for k, part in enumerate(sent, 1)
        ]
        values = call(sum_values_kernel, shape(256, 256, dtype=bf16), (), (kept, *came))
    with jax.named_scope("grad_tokens"):
        grad_tokens = call(
            token_gradient_kernel,
            shape(256, 2048, dtype=bf16),
            (core,),
            (cotangent, near, far, back_low, down),
        )
    return (values, grad_tokens, refreshed_down, scorer_a, refreshed_up)


def solution(mesh):
    fine = Mesh(mesh.devices.reshape(4, 2, 8, 2, 4), ("zh", "c", "y", "zl", "x"))
    tokens_at = ("zh", "c", "y", "zl")
    in_specs = (
        P(tokens_at, "x"),
        P(tokens_at, None),
        P("x", ("y", "zl")),
        P("x", ("y", "zl")),
        P("x", None),
        P(),
    )
    out_specs = (
        P(tokens_at, "x"),
        P(tokens_at, "x"),
        P("x", None),
        P(),
        P(None, "x"),
    )
    return jax.shard_map(body, mesh=fine, in_specs=in_specs, out_specs=out_specs, check_vma=False)
```

```python
import math

import jax
import jax.numpy as jnp
from jax import lax
from jax.experimental import pallas as pl
from jax.experimental.pallas import tpu as pltpu
from jax.sharding import Mesh
from jax.sharding import PartitionSpec as P

MODEL_WIDTH = 8192
QB = 128
INV_ROOT = 1.0 / math.sqrt(MODEL_WIDTH)

adapter_scale = 0.25
down_learning_rate = 1.0
up_learning_rate = 0.1
eps_norm = 1e-06

f32 = jnp.float32
bf16 = jnp.bfloat16
PLANE = ("zh", "y", "zl")
LIMIT = 32 * 1024 * 1024
WHOLE = 60 * 1024 * 1024

NN = (((1,), (0,)), ((), ()))
NT = (((1,), (1,)), ((), ()))
TN = (((0,), (0,)), ((), ()))


def dot(a, b, dims):
    return lax.dot_general(a, b, dims, preferred_element_type=f32)


def thirds(a):
    high = a.astype(bf16)
    rest = a - high.astype(f32)
    middle = rest.astype(bf16)
    return high, middle, (rest - middle.astype(f32)).astype(bf16)


def load(sources, places, sems):
    copies = [pltpu.make_async_copy(a, b, sems.at[i]) for i, (a, b) in enumerate(zip(sources, places))]
    for copy in copies:
        copy.start()
    for copy in copies:
        copy.wait()


def cost(mib):
    return pl.CostEstimate(flops=0, bytes_accessed=mib << 20, transcendentals=0)


def call(kernel, outs, scalars, stored, arrays, limit=LIMIT, after=()):
    first = len(scalars)
    count = len(stored)
    last = first + count + len(arrays)

    def loaded(*refs):
        refs = refs[:last] + refs[last + len(after) :]
        sources, others = refs[first : first + count], refs[first + count :]
        if count:
            *others, sems = others
            places = others[len(others) - count :]
            load(sources, places, sems)
            others = others[: len(others) - count]
            kernel(*refs[:first], *places, *others)
        else:
            kernel(*refs)

    scratch = [pltpu.VMEM(a.shape, a.dtype) for a in stored]
    return pl.pallas_call(
        loaded,
        out_shape=outs,
        in_specs=[pl.BlockSpec(memory_space=pltpu.SMEM)] * first
        + [pl.BlockSpec(memory_space=pltpu.HBM)] * count
        + [pl.BlockSpec(memory_space=pltpu.VMEM)] * len(arrays)
        + [pl.BlockSpec(memory_space=pl.ANY)] * len(after),
        out_specs=jax.tree.map(lambda _: pl.BlockSpec(memory_space=pltpu.VMEM), outs),
        scratch_shapes=scratch + [pltpu.SemaphoreType.DMA((count,))] * (count > 0),
        compiler_params=pltpu.CompilerParams(vmem_limit_bytes=limit),
        cost_estimate=cost(4),
    )(*scalars, *stored, *arrays, *after)


def shape(*dims, dtype=f32):
    return jax.ShapeDtypeStruct(dims, dtype)


def halves(core, width):
    first = pl.multiple_of(core * width, width)
    return pl.ds(first, width), pl.ds(pl.multiple_of(width - first, width), width)


def store_tiles(ref, wide, first):
    rows, columns = wide.shape[0] // 8, wide.shape[1] // 128
    for i in range(rows):
        for j in range(columns):
            ref[i * columns + j, first : first + 8] = wide[
                8 * i : 8 * i + 8, 128 * j : 128 * j + 128
            ]


def load_tiles(ref):
    halves_of = [ref[i].astype(f32) for i in range(64)]
    return [
        jnp.concatenate(
            [
                jnp.concatenate([halves_of[8 * i + j][first : first + 8] for j in range(8)], axis=1)
                for i in range(8)
            ],
            axis=0,
        )
        for first in (0, 8)
    ]


def dequant_kernel(core, codes, scales, out):
    wide = scales[...].astype(f32).T
    count = wide.shape[1] // 2
    mine = jnp.where(core[0] == 0, wide[:, :count], wide[:, count:])
    own, _ = halves(core[0], codes.shape[1] // 2)
    for j in range(count):
        block = codes[:, pl.ds(pl.multiple_of(own.start + QB * j, QB), QB)].astype(f32)
        out[:, QB * j : QB * j + QB] = (block * mine[:, j : j + 1]).astype(bf16)


def pair_kernel(low_first, mine, theirs, out):
    count = mine.shape[0]
    first = low_first[0] == 0
    out[:count] = jnp.where(first, mine[...], theirs[...])
    out[count:] = jnp.where(first, theirs[...], mine[...])


def gradients_kernel(
    core, tokens, cotangent, down, up, low_ref, rank_ref, send_ref, parts_ref, mark_ref
):
    mark_ref[...] = jnp.zeros(mark_ref.shape, f32)
    wide = cotangent[...]
    high, middle, low = thirds(up[...])
    back = dot(wide, low, NT) + dot(wide, middle, NT) + dot(wide, high, NT)
    back_low = (adapter_scale * back).astype(bf16)
    low_ref[...] = back_low
    own, other = halves(core[0], tokens.shape[1] // 2)
    store_tiles(send_ref, dot(back_low, tokens[:, other], TN) * INV_ROOT, 0)
    store_tiles(parts_ref, dot(back_low, tokens[:, own], TN) * INV_ROOT, 0)
    rank = dot(tokens[...], down[...].astype(bf16), NT) * INV_ROOT
    rank_ref[...] = rank
    high, middle, low = thirds(rank)
    up_grad = dot(low, wide, TN) + dot(middle, wide, TN) + dot(high, wide, TN)
    store_tiles(parts_ref, adapter_scale * up_grad, 8)


def parts_kernel(parts, arrived, out):
    for i in range(out.shape[0]):
        both = jnp.concatenate([parts[i, :8] + arrived[i], parts[i, 8:]], axis=0)
        out[i] = both.astype(bf16)


def total_kernel(parts, out):
    total = parts[0].astype(f32)
    for i in range(1, parts.shape[0]):
        total = total + parts[i].astype(f32)
    low = total.astype(bf16)
    for i in range(parts.shape[0]):
        out[i] = low


def normed(grad):
    mean = jnp.mean(grad * grad, axis=0, keepdims=True)
    return grad * lax.rsqrt(mean + eps_norm)


def scorer_kernel(core, weight, down, gathered, out, raw_ref, same):
    del weight, same
    own, _ = halves(core[0], down.shape[1] // 2)
    grad, up_grad = load_tiles(gathered)
    raw_ref[...] = grad.astype(bf16)
    fresh = (down[:, own] - down_learning_rate * normed(grad)).astype(bf16)
    up_grad = up_grad.astype(bf16)
    for p in range(4):
        out[p, :64, :] = fresh
        for i in range(4):
            out[p, 64:, 256 * i : 256 * i + 256] = up_grad[
                16 * i : 16 * i + 16, 256 * p : 256 * p + 256
            ]


def scorer_rows(core, weight, down, gathered):
    stored, here = pl.BlockSpec(memory_space=pltpu.HBM), pl.BlockSpec(memory_space=pltpu.VMEM)
    return pl.pallas_call(
        scorer_kernel,
        out_shape=(
            shape(4, 80, 1024, dtype=bf16),
            shape(64, 1024, dtype=bf16),
            shape(*weight.shape, dtype=bf16),
        ),
        in_specs=[pl.BlockSpec(memory_space=pltpu.SMEM), stored, here, here],
        out_specs=(here, here, stored),
        input_output_aliases={1: 2},
        compiler_params=pltpu.CompilerParams(vmem_limit_bytes=LIMIT),
        cost_estimate=cost(4),
    )(core, weight, down, gathered)


def down_kernel(core, down, raw, raw_other, out, mark_ref):
    mark_ref[...] = jnp.zeros(mark_ref.shape, f32)
    own, other = halves(core[0], down.shape[1] // 2)
    out[:, own] = down[:, own] - down_learning_rate * normed(raw[...].astype(f32))
    out[:, other] = down[:, other] - down_learning_rate * normed(raw_other[...].astype(f32))


def part_sum(rows):
    wide = rows[0, 64:80, :].astype(f32)
    for p in range(1, 4):
        wide = wide + rows[p, 64:80, :].astype(f32)
    return jnp.concatenate([wide[:, 256 * i : 256 * i + 256] for i in range(4)], axis=0)


def finish_kernel(core, place, up, rows, rows_other, scorer_ref, up_ref):
    own, other = halves(core[0], 1024)
    for p in range(4):
        scorer_ref[:, pl.ds(pl.multiple_of(2048 * p + own.start, 1024), 1024)] = rows[p, :64, :]
        scorer_ref[:, pl.ds(pl.multiple_of(2048 * p + other.start, 1024), 1024)] = rows_other[p, :64, :]
    columns = pl.ds(pl.multiple_of(place[0] * 256, 256), 256)
    total = part_sum(rows) + part_sum(rows_other)
    up_ref[...] = up[:, columns] - up_learning_rate * normed(total)


def near_values_kernel(core, tokens, weight, rank, up, out):
    own, _ = halves(core[0], tokens.shape[1] // 2)
    branch = lax.dot_general(
        rank[...], up[...], NN, precision=lax.Precision.HIGHEST, preferred_element_type=f32
    )
    out[...] = dot(tokens[:, own], weight[...], NT) + adapter_scale * branch


def far_values_kernel(core, tokens, weight, near, rows, out, *scratch):
    *places, result, sems, sem = scratch
    _, other = halves(core[0], tokens.shape[1] // 2)
    load((tokens.at[:, other], weight, near, rows), places, sems)
    tokens_at, weight_at, near_at, rows_at = places
    low = (near_at[...] + dot(tokens_at[...], weight_at[...], NT)).astype(bf16)
    for p in range(4):
        result[p, :80, :] = rows_at[p]
        for i in range(4):
            result[p, 80:, 256 * i : 256 * i + 256] = low[64 * i : 64 * i + 64, 256 * p : 256 * p + 256]
    copy = pltpu.make_async_copy(result, out, sem)
    copy.start()
    copy.wait()


def far_values(core, tokens, weight, near, rows):
    stored = pl.BlockSpec(memory_space=pltpu.HBM)
    out = (rows.shape[0], rows.shape[1] + 64, rows.shape[2])
    return pl.pallas_call(
        far_values_kernel,
        out_shape=shape(*out, dtype=bf16),
        in_specs=[pl.BlockSpec(memory_space=pltpu.SMEM)] + [stored] * 4,
        out_specs=stored,
        scratch_shapes=[
            pltpu.VMEM((tokens.shape[0], tokens.shape[1] // 2), bf16),
            pltpu.VMEM(weight.shape, bf16),
            pltpu.VMEM(near.shape, f32),
            pltpu.VMEM(rows.shape, bf16),
            pltpu.VMEM(out, bf16),
            pltpu.SemaphoreType.DMA((4,)),
            pltpu.SemaphoreType.DMA,
        ],
        compiler_params=pltpu.CompilerParams(vmem_limit_bytes=WHOLE),
        cost_estimate=cost(8),
    )(core, tokens, weight, near, rows)


def sum_values_kernel(came, mark_1, mark_2, out, same):
    del mark_1, mark_2, same
    for i in range(4):
        total = came[0, 80:, 256 * i : 256 * i + 256].astype(f32)
        for p in range(1, 4):
            total = total + came[p, 80:, 256 * i : 256 * i + 256].astype(f32)
        out[64 * i : 64 * i + 64, :] = total.astype(bf16)


def sum_values(came, mark_1, mark_2):
    here, anywhere = pl.BlockSpec(memory_space=pltpu.VMEM), pl.BlockSpec(memory_space=pl.ANY)
    return pl.pallas_call(
        sum_values_kernel,
        out_shape=(shape(256, 256, dtype=bf16), shape(*came.shape, dtype=bf16)),
        in_specs=[here, anywhere, anywhere],
        out_specs=(here, here),
        input_output_aliases={0: 1},
        compiler_params=pltpu.CompilerParams(vmem_limit_bytes=LIMIT),
        cost_estimate=cost(4),
    )(came, mark_1, mark_2)


def token_gradients_kernel(core, cotangent, low, down, near, far, out, mark_ref, *scratch):
    mark_ref[...] = jnp.zeros(mark_ref.shape, f32)
    wide, thin, master, matrices, result, sems, out_sems = scratch
    width = matrices.shape[2]
    sources = (cotangent, low, down, near, far)
    places = (wide, thin, master, matrices.at[0], matrices.at[1])
    loads = [pltpu.make_async_copy(a, b, sems.at[i]) for i, (a, b) in enumerate(zip(sources, places))]
    for copy in loads:
        copy.start()
    for copy in loads[:3]:
        copy.wait()
    stores = []
    for h, place in enumerate(halves(core[0], width)):
        loads[3 + h].wait()
        for q in range(2):
            step = width // 2
            columns = pl.ds(pl.multiple_of(place.start + step * q, step), step)
            part = pl.ds(step * q, step)
            beside = dot(thin[...], master[:, columns].astype(bf16), NN) * INV_ROOT
            result[h, :, part] = (dot(wide[...], matrices[h, :, part], NN) + beside).astype(bf16)
            stores.append(
                pltpu.make_async_copy(
                    result.at[h, :, part], out.at[:, columns], out_sems.at[2 * h + q]
                )
            )
            stores[-1].start()
    for copy in stores:
        copy.wait()


def token_gradients(core, cotangent, low, down, near, far):
    rows, columns = cotangent.shape[0], down.shape[1]
    stored = pl.BlockSpec(memory_space=pltpu.HBM)
    return pl.pallas_call(
        token_gradients_kernel,
        out_shape=(shape(rows, columns, dtype=bf16), shape(8, 128)),
        in_specs=[pl.BlockSpec(memory_space=pltpu.SMEM)] + [stored] * 5,
        out_specs=(stored, pl.BlockSpec(memory_space=pltpu.VMEM)),
        scratch_shapes=[
            pltpu.VMEM(cotangent.shape, bf16),
            pltpu.VMEM(low.shape, bf16),
            pltpu.VMEM(down.shape, f32),
            pltpu.VMEM((2, *near.shape), bf16),
            pltpu.VMEM((2, rows, columns // 2), bf16),
            pltpu.SemaphoreType.DMA((5,)),
            pltpu.SemaphoreType.DMA((4,)),
        ],
        compiler_params=pltpu.CompilerParams(vmem_limit_bytes=WHOLE),
        cost_estimate=cost(8),
    )(core, cotangent, low, down, near, far)


def body(tokens, cotangent, codes, scales, adapter_down, adapter_up):
    core_at = lax.axis_index("c")
    core = core_at.astype(jnp.int32).reshape(1)
    place = lax.axis_index("x").astype(jnp.int32).reshape(1)
    down = adapter_down.T
    swap = [(0, 1), (1, 0)]
    half = codes.shape[0] // 2

    mark = shape(8, 128)
    z_low = lax.axis_index("zl").astype(jnp.int32).reshape(1)

    with jax.named_scope("dequant"):
        mine = call(
            dequant_kernel,
            shape(codes.shape[1], half, dtype=bf16),
            (core,),
            (codes.T, scales),
            (),
            WHOLE,
        )
        theirs = lax.ppermute(mine, "zl", swap)
    with jax.named_scope("gradients"):
        back_low, rank, send, parts, begun = call(
            gradients_kernel,
            (
                shape(256, 64, dtype=bf16),
                shape(256, 64),
                shape(64, 8, 128),
                shape(64, 16, 128),
                mark,
            ),
            (core,),
            (tokens, cotangent, down, adapter_up),
            (),
            WHOLE,
        )
        arrived = lax.ppermute(send, "c", swap)
    with jax.named_scope("weight_gather"):
        pair = call(
            pair_kernel,
            shape(128, half, dtype=bf16),
            (z_low,),
            (),
            (mine, theirs),
            after=(begun,),
        )
        weight = lax.all_gather(pair, "y", axis=0, tiled=True)
    with jax.named_scope("plane_sum"):
        parts = call(parts_kernel, shape(64, 16, 128, dtype=bf16), (), (), (parts, arrived))
        parts = lax.all_to_all(parts, PLANE, 0, 0, tiled=True)
        total = call(total_kernel, shape(64, 16, 128, dtype=bf16), (), (), (parts,))
        gathered = lax.all_to_all(total, PLANE, 0, 0, tiled=True)
    with jax.named_scope("weight_swap"):
        rows, raw, near = scorer_rows(core, weight, down, gathered)
        far = lax.ppermute(near, "c", swap)
        raw_other = lax.ppermute(raw, "c", swap)
    with jax.named_scope("values"):
        near_part = call(
            near_values_kernel, shape(256, 1024), (core,), (tokens, near, rank, adapter_up), (), WHOLE
        )
        sent = far_values(core, tokens, far, near_part, rows)
        came = lax.all_to_all(sent, "x", 0, 0, tiled=True)
    with jax.named_scope("refresh"):
        refreshed_down, refreshed = call(
            down_kernel, (shape(64, 2048), mark), (core,), (), (down, raw, raw_other)
        )
        refreshed_down = refreshed_down.T
    with jax.named_scope("grad_tokens"):
        grad_tokens, turned = token_gradients(core, cotangent, back_low, down, near, far)
    with jax.named_scope("values"):
        values, came = sum_values(came, turned, refreshed)
    with jax.named_scope("refresh"):
        came_other = lax.ppermute(came, "c", swap)
        scorer_a, refreshed_up = call(
            finish_kernel,
            (shape(64, 8192, dtype=bf16), shape(64, 256)),
            (core, place),
            (),
            (adapter_up, came, came_other),
        )
        scorer_a = scorer_a.T
    return (values, grad_tokens, refreshed_down, scorer_a, refreshed_up)


def solution(mesh):
    fine = Mesh(mesh.devices.reshape(4, 2, 8, 2, 4), ("zh", "c", "y", "zl", "x"))
    tokens_at = ("zh", "c", "y", "zl")
    in_specs = (
        P(tokens_at, "x"),
        P(tokens_at, None),
        P("x", ("y", "zl")),
        P("x", ("y", "zl")),
        P("x", None),
        P(),
    )
    out_specs = (
        P(tokens_at, "x"),
        P(tokens_at, "x"),
        P("x", None),
        P(),
        P(None, "x"),
    )
    return jax.shard_map(body, mesh=fine, in_specs=in_specs, out_specs=out_specs, check_vma=False)
```

```python
import math

import jax
import jax.numpy as jnp
from jax import lax
from jax.experimental import pallas as pl
from jax.experimental.pallas import tpu as pltpu
from jax.sharding import Mesh
from jax.sharding import PartitionSpec as P

MODEL_WIDTH = 8192
QB = 128
INV_ROOT = 1.0 / math.sqrt(MODEL_WIDTH)

adapter_scale = 0.25
down_learning_rate = 1.0
up_learning_rate = 0.1
eps_norm = 1e-06

f32 = jnp.float32
bf16 = jnp.bfloat16
PLANE = ("zh", "y", "zl")
LIMIT = 32 * 1024 * 1024
WHOLE = 60 * 1024 * 1024

NN = (((1,), (0,)), ((), ()))
NT = (((1,), (1,)), ((), ()))
TN = (((0,), (0,)), ((), ()))


def dot(a, b, dims):
    return lax.dot_general(a, b, dims, preferred_element_type=f32)


def thirds(a):
    high = a.astype(bf16)
    rest = a - high.astype(f32)
    middle = rest.astype(bf16)
    return high, middle, (rest - middle.astype(f32)).astype(bf16)


def load(sources, places, sems):
    copies = [pltpu.make_async_copy(a, b, sems.at[i]) for i, (a, b) in enumerate(zip(sources, places))]
    for copy in copies:
        copy.start()
    for copy in copies:
        copy.wait()


def cost(mib):
    return pl.CostEstimate(flops=0, bytes_accessed=mib << 20, transcendentals=0)


def call(kernel, outs, scalars, stored, arrays, limit=LIMIT, after=()):
    first = len(scalars)
    count = len(stored)
    last = first + count + len(arrays)

    def loaded(*refs):
        refs = refs[:last] + refs[last + len(after) :]
        sources, others = refs[first : first + count], refs[first + count :]
        if count:
            *others, sems = others
            places = others[len(others) - count :]
            load(sources, places, sems)
            others = others[: len(others) - count]
            kernel(*refs[:first], *places, *others)
        else:
            kernel(*refs)

    scratch = [pltpu.VMEM(a.shape, a.dtype) for a in stored]
    return pl.pallas_call(
        loaded,
        out_shape=outs,
        in_specs=[pl.BlockSpec(memory_space=pltpu.SMEM)] * first
        + [pl.BlockSpec(memory_space=pltpu.HBM)] * count
        + [pl.BlockSpec(memory_space=pltpu.VMEM)] * len(arrays)
        + [pl.BlockSpec(memory_space=pltpu.SMEM)] * len(after),
        out_specs=jax.tree.map(
            lambda a: pl.BlockSpec(memory_space=pltpu.SMEM if a.shape == (1,) else pltpu.VMEM), outs
        ),
        scratch_shapes=scratch + [pltpu.SemaphoreType.DMA((count,))] * (count > 0),
        compiler_params=pltpu.CompilerParams(vmem_limit_bytes=limit),
        cost_estimate=cost(4),
    )(*scalars, *stored, *arrays, *after)


def shape(*dims, dtype=f32):
    return jax.ShapeDtypeStruct(dims, dtype)


def halves(core, width):
    first = pl.multiple_of(core * width, width)
    return pl.ds(first, width), pl.ds(pl.multiple_of(width - first, width), width)


def store_tiles(ref, wide, first):
    rows, columns = wide.shape[0] // 8, wide.shape[1] // 128
    for i in range(rows):
        for j in range(columns):
            ref[i * columns + j, first : first + 8] = wide[
                8 * i : 8 * i + 8, 128 * j : 128 * j + 128
            ]


def load_tiles(ref):
    halves_of = [ref[i].astype(f32) for i in range(64)]
    return [
        jnp.concatenate(
            [
                jnp.concatenate([halves_of[8 * i + j][first : first + 8] for j in range(8)], axis=1)
                for i in range(8)
            ],
            axis=0,
        )
        for first in (0, 8)
    ]


def dequant_kernel(core, codes, scales, out):
    wide = scales[...].astype(f32).T
    count = wide.shape[1] // 2
    mine = jnp.where(core[0] == 0, wide[:, :count], wide[:, count:])
    own, _ = halves(core[0], codes.shape[1] // 2)
    for j in range(count):
        block = codes[:, pl.ds(pl.multiple_of(own.start + QB * j, QB), QB)].astype(f32)
        out[:, QB * j : QB * j + QB] = (block * mine[:, j : j + 1]).astype(bf16)


def pair_kernel(low_first, mine, theirs, out):
    count = mine.shape[0]
    first = low_first[0] == 0
    out[:count] = jnp.where(first, mine[...], theirs[...])
    out[count:] = jnp.where(first, theirs[...], mine[...])


def gradients_kernel(
    core, tokens, cotangent, down, up, low_ref, rank_ref, send_ref, parts_ref, mark
):
    mark[0] = 0
    wide = cotangent[...]
    high, middle, low = thirds(up[...])
    back = dot(wide, low, NT) + dot(wide, middle, NT) + dot(wide, high, NT)
    back_low = (adapter_scale * back).astype(bf16)
    low_ref[...] = back_low
    own, other = halves(core[0], tokens.shape[1] // 2)
    store_tiles(send_ref, dot(back_low, tokens[:, other], TN) * INV_ROOT, 0)
    store_tiles(parts_ref, dot(back_low, tokens[:, own], TN) * INV_ROOT, 0)
    rank = dot(down[...].astype(bf16), tokens[...], NT) * INV_ROOT
    rank_ref[...] = rank
    high, middle, low = thirds(rank)
    up_grad = dot(low, wide, NN) + dot(middle, wide, NN) + dot(high, wide, NN)
    store_tiles(parts_ref, adapter_scale * up_grad, 8)


def parts_kernel(parts, arrived, out):
    for i in range(out.shape[0]):
        both = jnp.concatenate([parts[i, :8] + arrived[i], parts[i, 8:]], axis=0)
        out[i] = both.astype(bf16)


def total_kernel(parts, out):
    total = parts[0].astype(f32)
    for i in range(1, parts.shape[0]):
        total = total + parts[i].astype(f32)
    low = total.astype(bf16)
    for i in range(parts.shape[0]):
        out[i] = low


def normed(grad):
    mean = jnp.mean(grad * grad, axis=0, keepdims=True)
    return grad * lax.rsqrt(mean + eps_norm)


def scorer_kernel(core, weight, down, gathered, out, raw_ref, same):
    del weight, same
    own, _ = halves(core[0], down.shape[1] // 2)
    grad, up_grad = load_tiles(gathered)
    raw_ref[...] = grad.astype(bf16)
    fresh = (down[:, own] - down_learning_rate * normed(grad)).astype(bf16)
    up_grad = up_grad.astype(bf16)
    for p in range(4):
        out[p, :64, :] = fresh
        for i in range(4):
            out[p, 64:, 256 * i : 256 * i + 256] = up_grad[
                16 * i : 16 * i + 16, 256 * p : 256 * p + 256
            ]


def scorer_rows(core, weight, down, gathered):
    stored, here = pl.BlockSpec(memory_space=pltpu.HBM), pl.BlockSpec(memory_space=pltpu.VMEM)
    return pl.pallas_call(
        scorer_kernel,
        out_shape=(
            shape(4, 80, 1024, dtype=bf16),
            shape(64, 1024, dtype=bf16),
            shape(*weight.shape, dtype=bf16),
        ),
        in_specs=[pl.BlockSpec(memory_space=pltpu.SMEM), stored, here, here],
        out_specs=(here, here, stored),
        input_output_aliases={1: 2},
        compiler_params=pltpu.CompilerParams(vmem_limit_bytes=LIMIT),
        cost_estimate=cost(4),
    )(core, weight, down, gathered)


def down_kernel(core, down, raw, raw_other, out):
    own, other = halves(core[0], down.shape[1] // 2)
    out[:, own] = down[:, own] - down_learning_rate * normed(raw[...].astype(f32))
    out[:, other] = down[:, other] - down_learning_rate * normed(raw_other[...].astype(f32))


def part_sum(rows):
    wide = rows[0, 64:, :].astype(f32)
    for p in range(1, 4):
        wide = wide + rows[p, 64:, :].astype(f32)
    return jnp.concatenate([wide[:, 256 * i : 256 * i + 256] for i in range(4)], axis=0)


def finish_kernel(core, place, up, rows, rows_other, scorer_ref, up_ref):
    own, other = halves(core[0], 1024)
    for p in range(4):
        scorer_ref[:, pl.ds(pl.multiple_of(2048 * p + own.start, 1024), 1024)] = rows[p, :64, :]
        scorer_ref[:, pl.ds(pl.multiple_of(2048 * p + other.start, 1024), 1024)] = rows_other[p, :64, :]
    columns = pl.ds(pl.multiple_of(place[0] * 256, 256), 256)
    total = part_sum(rows) + part_sum(rows_other)
    up_ref[...] = up[:, columns] - up_learning_rate * normed(total)


def values_kernel(core, tokens, near, far, rank, up, out, mark):
    mark[0] = 0
    own, other = halves(core[0], tokens.shape[1] // 2)
    high, middle, low = thirds(adapter_scale * rank[...])
    thin = jnp.concatenate([low, middle, high, middle, high, high], axis=0)
    high, middle, low = thirds(up[...])
    tall = jnp.concatenate([high, middle, low, high, middle, high], axis=0)
    total = dot(near[...], tokens[:, own], NT) + dot(far[...], tokens[:, other], NT)
    total = (total + dot(tall, thin, TN)).astype(bf16)
    for p in range(4):
        out[p] = total[256 * p : 256 * p + 256]


def sum_values_kernel(came, out):
    total = came[0].astype(f32)
    for p in range(1, 4):
        total = total + came[p].astype(f32)
    out[...] = total.T.astype(bf16)


def copy_kernel(rows, out):
    out[...] = rows[...]


def token_gradients_kernel(core, cotangent, low, down, near, far, out, mark):
    mark[0] = 0
    width = near.shape[1]
    for place, weight in zip(halves(core[0], width), (near, far)):
        beside = dot(low[...], down[:, place].astype(bf16), NN) * INV_ROOT
        out[:, place] = (dot(cotangent[...], weight[...], NN) + beside).astype(bf16)


def body(tokens, cotangent, codes, scales, adapter_down, adapter_up):
    core_at = lax.axis_index("c")
    core = core_at.astype(jnp.int32).reshape(1)
    place = lax.axis_index("x").astype(jnp.int32).reshape(1)
    down = adapter_down.T
    swap = [(0, 1), (1, 0)]
    half = codes.shape[0] // 2

    mark = shape(1, dtype=jnp.int32)
    z_low = lax.axis_index("zl").astype(jnp.int32).reshape(1)

    with jax.named_scope("dequant"):
        mine = call(
            dequant_kernel,
            shape(codes.shape[1], half, dtype=bf16),
            (core,),
            (codes.T, scales),
            (),
            WHOLE,
        )
        theirs = lax.ppermute(mine, "zl", swap)
    with jax.named_scope("gradients"):
        back_low, rank, send, parts, begun = call(
            gradients_kernel,
            (
                shape(256, 64, dtype=bf16),
                shape(64, 256),
                shape(64, 8, 128),
                shape(64, 16, 128),
                mark,
            ),
            (core,),
            (tokens, cotangent, down, adapter_up),
            (),
            WHOLE,
        )
        arrived = lax.ppermute(send, "c", swap)
    with jax.named_scope("weight_gather"):
        pair = call(
            pair_kernel,
            shape(128, half, dtype=bf16),
            (z_low,),
            (),
            (mine, theirs),
            after=(begun,),
        )
        weight = lax.all_gather(pair, "y", axis=0, tiled=True)
    with jax.named_scope("plane_sum"):
        parts = call(parts_kernel, shape(64, 16, 128, dtype=bf16), (), (), (parts, arrived))
        parts = lax.all_to_all(parts, PLANE, 0, 0, tiled=True)
        total = call(total_kernel, shape(64, 16, 128, dtype=bf16), (), (), (parts,))
        gathered = lax.all_to_all(total, PLANE, 0, 0, tiled=True)
    with jax.named_scope("refresh"):
        rows, raw, near = scorer_rows(core, weight, down, gathered)
        rows = lax.all_to_all(rows, "x", 0, 0, tiled=True)
    with jax.named_scope("values"):
        far = lax.ppermute(near, "c", swap)
        sent, whole = call(
            values_kernel,
            (shape(4, 256, 256, dtype=bf16), mark),
            (core,),
            (),
            (tokens, near, far, rank, adapter_up),
        )
        came = lax.all_to_all(sent, "x", 0, 0, tiled=True)
        values = call(sum_values_kernel, shape(256, 256, dtype=bf16), (), (), (came,))
    with jax.named_scope("grad_tokens"):
        grad_tokens, turned = call(
            token_gradients_kernel,
            (shape(256, 2048, dtype=bf16), mark),
            (core,),
            (),
            (cotangent, back_low, down, near, far),
            after=(whole,),
        )
    with jax.named_scope("refresh"):
        raw_other = lax.ppermute(raw, "c", swap)
        refreshed_down = call(
            down_kernel, shape(64, 2048), (core,), (), (down, raw, raw_other), after=(whole,)
        ).T
        rows = call(copy_kernel, shape(*rows.shape, dtype=bf16), (), (), (rows,), after=(turned,))
        rows_other = lax.ppermute(rows, "c", swap)
        scorer_a, refreshed_up = call(
            finish_kernel,
            (shape(64, 8192, dtype=bf16), shape(64, 256)),
            (core, place),
            (),
            (adapter_up, rows, rows_other),
        )
        scorer_a = scorer_a.T
    return (values, grad_tokens, refreshed_down, scorer_a, refreshed_up)


def solution(mesh):
    fine = Mesh(mesh.devices.reshape(4, 2, 8, 2, 4), ("zh", "c", "y", "zl", "x"))
    tokens_at = ("zh", "c", "y", "zl")
    in_specs = (
        P(tokens_at, "x"),
        P(tokens_at, None),
        P("x", ("y", "zl")),
        P("x", ("y", "zl")),
        P("x", None),
        P(),
    )
    out_specs = (
        P(tokens_at, "x"),
        P(tokens_at, "x"),
        P("x", None),
        P(),
        P(None, "x"),
    )
    return jax.shard_map(body, mesh=fine, in_specs=in_specs, out_specs=out_specs, check_vma=False)
```

```python
import math

import jax
import jax.numpy as jnp
from jax import lax
from jax.experimental import pallas as pl
from jax.experimental.pallas import tpu as pltpu
from jax.sharding import Mesh
from jax.sharding import PartitionSpec as P

MODEL_WIDTH = 8192
QB = 128
INV_ROOT = 1.0 / math.sqrt(MODEL_WIDTH)

adapter_scale = 0.25
down_learning_rate = 1.0
up_learning_rate = 0.1
eps_norm = 1e-06

f32 = jnp.float32
bf16 = jnp.bfloat16
PLANE = ("zh", "y", "zl")
LIMIT = 32 * 1024 * 1024
WHOLE = 60 * 1024 * 1024

NN = (((1,), (0,)), ((), ()))
NT = (((1,), (1,)), ((), ()))
TN = (((0,), (0,)), ((), ()))


def dot(a, b, dims):
    return lax.dot_general(a, b, dims, preferred_element_type=f32)


def thirds(a):
    high = a.astype(bf16)
    rest = a - high.astype(f32)
    middle = rest.astype(bf16)
    return high, middle, (rest - middle.astype(f32)).astype(bf16)


def load(sources, places, sems):
    copies = [pltpu.make_async_copy(a, b, sems.at[i]) for i, (a, b) in enumerate(zip(sources, places))]
    for copy in copies:
        copy.start()
    for copy in copies:
        copy.wait()


def cost(mib):
    return pl.CostEstimate(flops=0, bytes_accessed=mib << 20, transcendentals=0)


def call(kernel, outs, scalars, stored, arrays, limit=LIMIT, after=()):
    first = len(scalars)
    count = len(stored)
    last = first + count + len(arrays)

    def loaded(*refs):
        refs = refs[:last] + refs[last + len(after) :]
        sources, others = refs[first : first + count], refs[first + count :]
        if count:
            *others, sems = others
            places = others[len(others) - count :]
            load(sources, places, sems)
            others = others[: len(others) - count]
            kernel(*refs[:first], *places, *others)
        else:
            kernel(*refs)

    scratch = [pltpu.VMEM(a.shape, a.dtype) for a in stored]
    return pl.pallas_call(
        loaded,
        out_shape=outs,
        in_specs=[pl.BlockSpec(memory_space=pltpu.SMEM)] * first
        + [pl.BlockSpec(memory_space=pltpu.HBM)] * count
        + [pl.BlockSpec(memory_space=pltpu.VMEM)] * len(arrays)
        + [pl.BlockSpec(memory_space=pltpu.SMEM)] * len(after),
        out_specs=jax.tree.map(
            lambda a: pl.BlockSpec(memory_space=pltpu.SMEM if a.shape == (1,) else pltpu.VMEM), outs
        ),
        scratch_shapes=scratch + [pltpu.SemaphoreType.DMA((count,))] * (count > 0),
        compiler_params=pltpu.CompilerParams(vmem_limit_bytes=limit),
        cost_estimate=cost(4),
    )(*scalars, *stored, *arrays, *after)


def shape(*dims, dtype=f32):
    return jax.ShapeDtypeStruct(dims, dtype)


def halves(core, width):
    first = pl.multiple_of(core * width, width)
    return pl.ds(first, width), pl.ds(pl.multiple_of(width - first, width), width)


def store_tiles(ref, wide, first):
    rows, columns = wide.shape[0] // 8, wide.shape[1] // 128
    for i in range(rows):
        for j in range(columns):
            ref[i * columns + j, first : first + 8] = wide[
                8 * i : 8 * i + 8, 128 * j : 128 * j + 128
            ]


def load_tiles(ref):
    halves_of = [ref[i].astype(f32) for i in range(64)]
    return [
        jnp.concatenate(
            [
                jnp.concatenate([halves_of[8 * i + j][first : first + 8] for j in range(8)], axis=1)
                for i in range(8)
            ],
            axis=0,
        )
        for first in (0, 8)
    ]


def dequant_kernel(core, codes, scales, out):
    wide = scales[...].astype(f32).T
    count = wide.shape[1] // 2
    mine = jnp.where(core[0] == 0, wide[:, :count], wide[:, count:])
    own, _ = halves(core[0], codes.shape[1] // 2)
    for j in range(count):
        block = codes[:, pl.ds(pl.multiple_of(own.start + QB * j, QB), QB)].astype(f32)
        out[:, QB * j : QB * j + QB] = (block * mine[:, j : j + 1]).astype(bf16)


def pair_kernel(low_first, mine, theirs, out):
    count = mine.shape[0]
    first = low_first[0] == 0
    out[:count] = jnp.where(first, mine[...], theirs[...])
    out[count:] = jnp.where(first, theirs[...], mine[...])


def down_gradient_kernel(core, tokens, cotangent, up, low_ref, send_ref, keep_ref, mark):
    mark[0] = 0
    wide = cotangent[...]
    high, middle, low = thirds(up[...])
    back = dot(wide, low, NT) + dot(wide, middle, NT) + dot(wide, high, NT)
    back_low = (adapter_scale * back).astype(bf16)
    low_ref[...] = back_low
    own, other = halves(core[0], tokens.shape[1] // 2)
    store_tiles(send_ref, dot(back_low, tokens[:, other], TN) * INV_ROOT, 0)
    store_tiles(keep_ref, dot(back_low, tokens[:, own], TN) * INV_ROOT, 0)


def up_gradient_kernel(tokens, cotangent, down, tiles_ref):
    wide = cotangent[...]
    rank = dot(down[...].astype(bf16), tokens[...], NT) * INV_ROOT
    high, middle, low = thirds(rank)
    up_grad = dot(low, wide, NN) + dot(middle, wide, NN) + dot(high, wide, NN)
    store_tiles(tiles_ref, adapter_scale * up_grad, 0)


def parts_kernel(keep, tiles, arrived, out):
    for i in range(out.shape[0]):
        both = jnp.concatenate([keep[i] + arrived[i], tiles[i]], axis=0)
        out[i] = both.astype(bf16)


def total_kernel(parts, out):
    total = parts[0].astype(f32)
    for i in range(1, parts.shape[0]):
        total = total + parts[i].astype(f32)
    low = total.astype(bf16)
    for i in range(parts.shape[0]):
        out[i] = low


def normed(grad):
    mean = jnp.mean(grad * grad, axis=0, keepdims=True)
    return grad * lax.rsqrt(mean + eps_norm)


def scorer_kernel(core, weight, down, gathered, out, raw_ref, same):
    del weight, same
    own, _ = halves(core[0], down.shape[1] // 2)
    grad, up_grad = load_tiles(gathered)
    raw_ref[...] = grad.astype(bf16)
    fresh = (down[:, own] - down_learning_rate * normed(grad)).astype(bf16)
    up_grad = up_grad.astype(bf16)
    for p in range(4):
        out[p, :64, :] = fresh
        for i in range(4):
            out[p, 64:, 256 * i : 256 * i + 256] = up_grad[
                16 * i : 16 * i + 16, 256 * p : 256 * p + 256
            ]


def scorer_rows(core, weight, down, gathered):
    stored, here = pl.BlockSpec(memory_space=pltpu.HBM), pl.BlockSpec(memory_space=pltpu.VMEM)
    return pl.pallas_call(
        scorer_kernel,
        out_shape=(
            shape(4, 80, 1024, dtype=bf16),
            shape(64, 1024, dtype=bf16),
            shape(*weight.shape, dtype=bf16),
        ),
        in_specs=[pl.BlockSpec(memory_space=pltpu.SMEM), stored, here, here],
        out_specs=(here, here, stored),
        input_output_aliases={1: 2},
        compiler_params=pltpu.CompilerParams(vmem_limit_bytes=LIMIT),
        cost_estimate=cost(4),
    )(core, weight, down, gathered)


def down_kernel(core, down, raw, raw_other, out):
    own, other = halves(core[0], down.shape[1] // 2)
    out[:, own] = down[:, own] - down_learning_rate * normed(raw[...].astype(f32))
    out[:, other] = down[:, other] - down_learning_rate * normed(raw_other[...].astype(f32))


def part_sum(rows):
    wide = rows[0, 64:, :].astype(f32)
    for p in range(1, 4):
        wide = wide + rows[p, 64:, :].astype(f32)
    return jnp.concatenate([wide[:, 256 * i : 256 * i + 256] for i in range(4)], axis=0)


def finish_kernel(core, place, up, rows, rows_other, scorer_ref, up_ref):
    own, other = halves(core[0], 1024)
    for p in range(4):
        scorer_ref[:, pl.ds(pl.multiple_of(2048 * p + own.start, 1024), 1024)] = rows[p, :64, :]
        scorer_ref[:, pl.ds(pl.multiple_of(2048 * p + other.start, 1024), 1024)] = rows_other[p, :64, :]
    columns = pl.ds(pl.multiple_of(place[0] * 256, 256), 256)
    total = part_sum(rows) + part_sum(rows_other)
    up_ref[...] = up[:, columns] - up_learning_rate * normed(total)


def values_kernel(core, tokens, near, far, down, up, out, mark):
    mark[0] = 0
    own, other = halves(core[0], tokens.shape[1] // 2)
    rank = dot(down[...].astype(bf16), tokens[...], NT) * INV_ROOT
    high, middle, low = thirds(adapter_scale * rank)
    thin = jnp.concatenate([low, middle, high, middle, high, high], axis=0)
    high, middle, low = thirds(up[...])
    tall = jnp.concatenate([high, middle, low, high, middle, high], axis=0)
    total = dot(near[...], tokens[:, own], NT) + dot(far[...], tokens[:, other], NT)
    total = (total + dot(tall, thin, TN)).astype(bf16)
    for p in range(4):
        out[p] = total[256 * p : 256 * p + 256]


def sum_values_kernel(came, out):
    total = came[0].astype(f32)
    for p in range(1, 4):
        total = total + came[p].astype(f32)
    out[...] = total.T.astype(bf16)


def copy_kernel(rows, out):
    out[...] = rows[...]


def token_gradients_kernel(core, cotangent, low, down, near, far, out, mark):
    mark[0] = 0
    width = near.shape[1]
    for place, weight in zip(halves(core[0], width), (near, far)):
        beside = dot(low[...], down[:, place].astype(bf16), NN) * INV_ROOT
        out[:, place] = (dot(cotangent[...], weight[...], NN) + beside).astype(bf16)


def body(tokens, cotangent, codes, scales, adapter_down, adapter_up):
    core_at = lax.axis_index("c")
    core = core_at.astype(jnp.int32).reshape(1)
    place = lax.axis_index("x").astype(jnp.int32).reshape(1)
    down = adapter_down.T
    swap = [(0, 1), (1, 0)]
    half = codes.shape[0] // 2

    mark = shape(1, dtype=jnp.int32)
    z_low = lax.axis_index("zl").astype(jnp.int32).reshape(1)

    with jax.named_scope("dequant"):
        mine = call(
            dequant_kernel,
            shape(codes.shape[1], half, dtype=bf16),
            (core,),
            (codes.T, scales),
            (),
            WHOLE,
        )
        theirs = lax.ppermute(mine, "zl", swap)
    with jax.named_scope("gradients"):
        back_low, send, keep, begun = call(
            down_gradient_kernel,
            (shape(256, 64, dtype=bf16), shape(64, 8, 128), shape(64, 8, 128), mark),
            (core,),
            (tokens, cotangent, adapter_up),
            (),
            WHOLE,
        )
        arrived = lax.ppermute(send, "c", swap)
        up_tiles = call(
            up_gradient_kernel, shape(64, 8, 128), (), (tokens, cotangent, down), (), WHOLE
        )
    with jax.named_scope("weight_gather"):
        pair = call(
            pair_kernel,
            shape(128, half, dtype=bf16),
            (z_low,),
            (),
            (mine, theirs),
            after=(begun,),
        )
        weight = lax.all_gather(pair, "y", axis=0, tiled=True)
    with jax.named_scope("plane_sum"):
        parts = call(
            parts_kernel, shape(64, 16, 128, dtype=bf16), (), (), (keep, up_tiles, arrived)
        )
        parts = lax.all_to_all(parts, PLANE, 0, 0, tiled=True)
        total = call(total_kernel, shape(64, 16, 128, dtype=bf16), (), (), (parts,))
        gathered = lax.all_to_all(total, PLANE, 0, 0, tiled=True)
    with jax.named_scope("refresh"):
        rows, raw, near = scorer_rows(core, weight, down, gathered)
        rows = lax.all_to_all(rows, "x", 0, 0, tiled=True)
    with jax.named_scope("values"):
        far = lax.ppermute(near, "c", swap)
        sent, whole = call(
            values_kernel,
            (shape(4, 256, 256, dtype=bf16), mark),
            (core,),
            (),
            (tokens, near, far, down, adapter_up),
        )
        came = lax.all_to_all(sent, "x", 0, 0, tiled=True)
        values = call(sum_values_kernel, shape(256, 256, dtype=bf16), (), (), (came,))
    with jax.named_scope("grad_tokens"):
        grad_tokens, turned = call(
            token_gradients_kernel,
            (shape(256, 2048, dtype=bf16), mark),
            (core,),
            (),
            (cotangent, back_low, down, near, far),
            after=(whole,),
        )
    with jax.named_scope("refresh"):
        raw_other = lax.ppermute(raw, "c", swap)
        refreshed_down = call(
            down_kernel, shape(64, 2048), (core,), (), (down, raw, raw_other), after=(whole,)
        ).T
        rows = call(copy_kernel, shape(*rows.shape, dtype=bf16), (), (), (rows,), after=(turned,))
        rows_other = lax.ppermute(rows, "c", swap)
        scorer_a, refreshed_up = call(
            finish_kernel,
            (shape(64, 8192, dtype=bf16), shape(64, 256)),
            (core, place),
            (),
            (adapter_up, rows, rows_other),
        )
        scorer_a = scorer_a.T
    return (values, grad_tokens, refreshed_down, scorer_a, refreshed_up)


def solution(mesh):
    fine = Mesh(mesh.devices.reshape(4, 2, 8, 2, 4), ("zh", "c", "y", "zl", "x"))
    tokens_at = ("zh", "c", "y", "zl")
    in_specs = (
        P(tokens_at, "x"),
        P(tokens_at, None),
        P("x", ("y", "zl")),
        P("x", ("y", "zl")),
        P("x", None),
        P(),
    )
    out_specs = (
        P(tokens_at, "x"),
        P(tokens_at, "x"),
        P("x", None),
        P(),
        P(None, "x"),
    )
    return jax.shard_map(body, mesh=fine, in_specs=in_specs, out_specs=out_specs, check_vma=False)
```

```python
import math

import jax
import jax.numpy as jnp
from jax import lax
from jax.experimental import pallas as pl
from jax.experimental.pallas import tpu as pltpu
from jax.sharding import Mesh
from jax.sharding import PartitionSpec as P

MODEL_WIDTH = 8192
QB = 128
INV_ROOT = 1.0 / math.sqrt(MODEL_WIDTH)

adapter_scale = 0.25
down_learning_rate = 1.0
up_learning_rate = 0.1
eps_norm = 1e-06

f32 = jnp.float32
bf16 = jnp.bfloat16
PLANE = ("zh", "y", "zl")
LIMIT = 32 * 1024 * 1024
WHOLE = 60 * 1024 * 1024

NN = (((1,), (0,)), ((), ()))
NT = (((1,), (1,)), ((), ()))
TN = (((0,), (0,)), ((), ()))


def dot(a, b, dims):
    return lax.dot_general(a, b, dims, preferred_element_type=f32)


def thirds(a):
    high = a.astype(bf16)
    rest = a - high.astype(f32)
    middle = rest.astype(bf16)
    return high, middle, (rest - middle.astype(f32)).astype(bf16)


def load(sources, places, sems):
    copies = [pltpu.make_async_copy(a, b, sems.at[i]) for i, (a, b) in enumerate(zip(sources, places))]
    for copy in copies:
        copy.start()
    for copy in copies:
        copy.wait()


def cost(mib):
    return pl.CostEstimate(flops=0, bytes_accessed=mib << 20, transcendentals=0)


def call(kernel, outs, scalars, stored, arrays, limit=LIMIT, after=()):
    first = len(scalars)
    count = len(stored)
    last = first + count + len(arrays)

    def loaded(*refs):
        refs = refs[:last] + refs[last + len(after) :]
        sources, others = refs[first : first + count], refs[first + count :]
        if count:
            *others, sems = others
            places = others[len(others) - count :]
            load(sources, places, sems)
            others = others[: len(others) - count]
            kernel(*refs[:first], *places, *others)
        else:
            kernel(*refs)

    scratch = [pltpu.VMEM(a.shape, a.dtype) for a in stored]
    return pl.pallas_call(
        loaded,
        out_shape=outs,
        in_specs=[pl.BlockSpec(memory_space=pltpu.SMEM)] * first
        + [pl.BlockSpec(memory_space=pltpu.HBM)] * count
        + [pl.BlockSpec(memory_space=pltpu.VMEM)] * len(arrays)
        + [pl.BlockSpec(memory_space=pltpu.SMEM)] * len(after),
        out_specs=jax.tree.map(
            lambda a: pl.BlockSpec(memory_space=pltpu.SMEM if a.shape == (1,) else pltpu.VMEM), outs
        ),
        scratch_shapes=scratch + [pltpu.SemaphoreType.DMA((count,))] * (count > 0),
        compiler_params=pltpu.CompilerParams(vmem_limit_bytes=limit),
        cost_estimate=cost(4),
    )(*scalars, *stored, *arrays, *after)


def shape(*dims, dtype=f32):
    return jax.ShapeDtypeStruct(dims, dtype)


def halves(core, width):
    first = pl.multiple_of(core * width, width)
    return pl.ds(first, width), pl.ds(pl.multiple_of(width - first, width), width)


def store_tiles(ref, wide, first):
    rows, columns = wide.shape[0] // 8, wide.shape[1] // 128
    for i in range(rows):
        for j in range(columns):
            ref[i * columns + j, first : first + 8] = wide[
                8 * i : 8 * i + 8, 128 * j : 128 * j + 128
            ]


def load_tiles(ref):
    halves_of = [ref[i].astype(f32) for i in range(64)]
    return [
        jnp.concatenate(
            [
                jnp.concatenate([halves_of[8 * i + j][first : first + 8] for j in range(8)], axis=1)
                for i in range(8)
            ],
            axis=0,
        )
        for first in (0, 8)
    ]


def dequant_kernel(core, codes, scales, out):
    wide = scales[...].astype(f32).T
    count = wide.shape[1] // 2
    mine = jnp.where(core[0] == 0, wide[:, :count], wide[:, count:])
    own, _ = halves(core[0], codes.shape[1] // 2)
    for j in range(count):
        block = codes[:, pl.ds(pl.multiple_of(own.start + QB * j, QB), QB)].astype(f32)
        out[:, QB * j : QB * j + QB] = (block * mine[:, j : j + 1]).astype(bf16)


def pair_kernel(low_first, mine, theirs, out):
    count = mine.shape[0]
    first = low_first[0] == 0
    out[:count] = jnp.where(first, mine[...], theirs[...])
    out[count:] = jnp.where(first, theirs[...], mine[...])


def down_gradient_kernel(core, tokens, cotangent, up, low_ref, send_ref, keep_ref, mark):
    mark[0] = 0
    wide = cotangent[...]
    high, middle, low = thirds(up[...])
    back = dot(wide, low, NT) + dot(wide, middle, NT) + dot(wide, high, NT)
    back_low = (adapter_scale * back).astype(bf16)
    low_ref[...] = back_low
    own, other = halves(core[0], tokens.shape[1] // 2)
    store_tiles(send_ref, dot(back_low, tokens[:, other], TN) * INV_ROOT, 0)
    store_tiles(keep_ref, dot(back_low, tokens[:, own], TN) * INV_ROOT, 0)


def up_gradient_kernel(tokens, cotangent, down, tiles_ref):
    wide = cotangent[...]
    rank = dot(down[...].astype(bf16), tokens[...], NT) * INV_ROOT
    high, middle, low = thirds(rank)
    up_grad = dot(low, wide, NN) + dot(middle, wide, NN) + dot(high, wide, NN)
    store_tiles(tiles_ref, adapter_scale * up_grad, 0)


def parts_kernel(keep, tiles, arrived, out):
    for i in range(out.shape[0]):
        both = jnp.concatenate([keep[i] + arrived[i], tiles[i]], axis=0)
        out[i] = both.astype(bf16)


def total_kernel(parts, out):
    total = parts[0].astype(f32)
    for i in range(1, parts.shape[0]):
        total = total + parts[i].astype(f32)
    low = total.astype(bf16)
    for i in range(parts.shape[0]):
        out[i] = low


def normed(grad):
    mean = jnp.mean(grad * grad, axis=0, keepdims=True)
    return grad * lax.rsqrt(mean + eps_norm)


def scorer_kernel(core, weight, down, gathered, out, raw_ref, same):
    del weight, same
    own, _ = halves(core[0], down.shape[1] // 2)
    grad, up_grad = load_tiles(gathered)
    raw_ref[...] = grad.astype(bf16)
    fresh = (down[:, own] - down_learning_rate * normed(grad)).astype(bf16)
    up_grad = up_grad.astype(bf16)
    for p in range(4):
        out[p, :64, :] = fresh
        for i in range(4):
            out[p, 64:, 256 * i : 256 * i + 256] = up_grad[
                16 * i : 16 * i + 16, 256 * p : 256 * p + 256
            ]


def scorer_rows(core, weight, down, gathered):
    stored, here = pl.BlockSpec(memory_space=pltpu.HBM), pl.BlockSpec(memory_space=pltpu.VMEM)
    return pl.pallas_call(
        scorer_kernel,
        out_shape=(
            shape(4, 80, 1024, dtype=bf16),
            shape(64, 1024, dtype=bf16),
            shape(*weight.shape, dtype=bf16),
        ),
        in_specs=[pl.BlockSpec(memory_space=pltpu.SMEM), stored, here, here],
        out_specs=(here, here, stored),
        input_output_aliases={1: 2},
        compiler_params=pltpu.CompilerParams(vmem_limit_bytes=LIMIT),
        cost_estimate=cost(4),
    )(core, weight, down, gathered)


def down_kernel(core, down, raw, raw_other, out):
    own, other = halves(core[0], down.shape[1] // 2)
    out[:, own] = down[:, own] - down_learning_rate * normed(raw[...].astype(f32))
    out[:, other] = down[:, other] - down_learning_rate * normed(raw_other[...].astype(f32))


def part_sum(rows):
    wide = rows[0, 64:, :].astype(f32)
    for p in range(1, 4):
        wide = wide + rows[p, 64:, :].astype(f32)
    return jnp.concatenate([wide[:, 256 * i : 256 * i + 256] for i in range(4)], axis=0)


def finish_kernel(core, place, up, rows, rows_other, scorer_ref, up_ref):
    own, other = halves(core[0], 1024)
    for p in range(4):
        scorer_ref[:, pl.ds(pl.multiple_of(2048 * p + own.start, 1024), 1024)] = rows[p, :64, :]
        scorer_ref[:, pl.ds(pl.multiple_of(2048 * p + other.start, 1024), 1024)] = rows_other[p, :64, :]
    columns = pl.ds(pl.multiple_of(place[0] * 256, 256), 256)
    total = part_sum(rows) + part_sum(rows_other)
    up_ref[...] = up[:, columns] - up_learning_rate * normed(total)


def values_kernel(core, tokens, near, far, down, up, out, mark):
    mark[0] = 0
    own, other = halves(core[0], tokens.shape[1] // 2)
    rank = dot(down[...].astype(bf16), tokens[...], NT) * INV_ROOT
    high, middle, low = thirds(adapter_scale * rank)
    thin = jnp.concatenate([low, middle, high, middle, high, high], axis=0)
    high, middle, low = thirds(up[...])
    tall = jnp.concatenate([high, middle, low, high, middle, high], axis=0)
    total = dot(near[...], tokens[:, own], NT) + dot(far[...], tokens[:, other], NT)
    total = (total + dot(tall, thin, TN)).astype(bf16)
    for p in range(4):
        out[p] = total[256 * p : 256 * p + 256]


def sum_values_kernel(came, out):
    total = came[0].astype(f32)
    for p in range(1, 4):
        total = total + came[p].astype(f32)
    out[...] = total.T.astype(bf16)


def copy_kernel(rows, out):
    out[...] = rows[...]


def token_gradients_kernel(core, cotangent, low, down, near, far, out, mark):
    mark[0] = 0
    width = near.shape[1]
    for place, weight in zip(halves(core[0], width), (near, far)):
        beside = dot(low[...], down[:, place].astype(bf16), NN) * INV_ROOT
        out[:, place] = (dot(cotangent[...], weight[...], NN) + beside).astype(bf16)


def body(tokens, cotangent, codes, scales, adapter_down, adapter_up):
    core_at = lax.axis_index("c")
    core = core_at.astype(jnp.int32).reshape(1)
    place = lax.axis_index("x").astype(jnp.int32).reshape(1)
    down = adapter_down.T
    swap = [(0, 1), (1, 0)]
    half = codes.shape[0] // 2

    mark = shape(1, dtype=jnp.int32)
    z_low = lax.axis_index("zl").astype(jnp.int32).reshape(1)

    with jax.named_scope("dequant"):
        mine = call(
            dequant_kernel,
            shape(codes.shape[1], half, dtype=bf16),
            (core,),
            (codes.T, scales),
            (),
            WHOLE,
        )
        theirs = lax.ppermute(mine, "zl", swap)
    with jax.named_scope("gradients"):
        back_low, send, keep, begun = call(
            down_gradient_kernel,
            (shape(256, 64, dtype=bf16), shape(64, 8, 128), shape(64, 8, 128), mark),
            (core,),
            (tokens, cotangent, adapter_up),
            (),
            WHOLE,
        )
        arrived = lax.ppermute(send, "c", swap)
        up_tiles = call(
            up_gradient_kernel, shape(64, 8, 128), (), (tokens, cotangent, down), (), WHOLE
        )
    with jax.named_scope("weight_gather"):
        pair = call(
            pair_kernel,
            shape(128, half, dtype=bf16),
            (z_low,),
            (),
            (mine, theirs),
            after=(begun,),
        )
        weight = lax.all_gather(pair, "y", axis=0, tiled=True)
    with jax.named_scope("plane_sum"):
        parts = call(
            parts_kernel, shape(64, 16, 128, dtype=bf16), (), (), (keep, up_tiles, arrived)
        )
        parts = lax.all_to_all(parts, PLANE, 0, 0, tiled=True)
        total = call(total_kernel, shape(64, 16, 128, dtype=bf16), (), (), (parts,))
        gathered = lax.all_to_all(total, PLANE, 0, 0, tiled=True)
    with jax.named_scope("refresh"):
        rows, raw, near = scorer_rows(core, weight, down, gathered)
        rows = lax.all_to_all(rows, "x", 0, 0, tiled=True)
    with jax.named_scope("values"):
        far = lax.ppermute(near, "c", swap)
        sent, whole = call(
            values_kernel,
            (shape(4, 256, 256, dtype=bf16), mark),
            (core,),
            (),
            (tokens, near, far, down, adapter_up),
        )
        came = lax.all_to_all(sent, "x", 0, 0, tiled=True)
        values = call(sum_values_kernel, shape(256, 256, dtype=bf16), (), (), (came,))
    with jax.named_scope("grad_tokens"):
        grad_tokens, turned = call(
            token_gradients_kernel,
            (shape(256, 2048, dtype=bf16), mark),
            (core,),
            (),
            (cotangent, back_low, down, near, far),
            after=(whole,),
        )
    with jax.named_scope("refresh"):
        raw_other = lax.ppermute(raw, "c", swap)
        refreshed_down = call(
            down_kernel, shape(64, 2048), (core,), (), (down, raw, raw_other), after=(whole,)
        ).T
        rows = call(copy_kernel, shape(*rows.shape, dtype=bf16), (), (), (rows,), after=(whole,))
        rows_other = lax.ppermute(rows, "c", swap)
        scorer_a, refreshed_up = call(
            finish_kernel,
            (shape(64, 8192, dtype=bf16), shape(64, 256)),
            (core, place),
            (),
            (adapter_up, rows, rows_other),
        )
        scorer_a = scorer_a.T
    return (values, grad_tokens, refreshed_down, scorer_a, refreshed_up)


def solution(mesh):
    fine = Mesh(mesh.devices.reshape(4, 2, 8, 2, 4), ("zh", "c", "y", "zl", "x"))
    tokens_at = ("zh", "c", "y", "zl")
    in_specs = (
        P(tokens_at, "x"),
        P(tokens_at, None),
        P("x", ("y", "zl")),
        P("x", ("y", "zl")),
        P("x", None),
        P(),
    )
    out_specs = (
        P(tokens_at, "x"),
        P(tokens_at, "x"),
        P("x", None),
        P(),
        P(None, "x"),
    )
    return jax.shard_map(body, mesh=fine, in_specs=in_specs, out_specs=out_specs, check_vma=False)
```
